256 devices in a mesh: lon: 64 (over z, y_lo, x), lat: 4 (over y_hi, core).
Axes of the slice: x: 4, y: 4 (y_hi: 2, y_lo: 2; y = y_hi * 2 + y_lo), z: 8, core: 2. Of those that a mesh axis runs over, the one named last changes fastest.
Arguments:
- tokens: bfloat16 [2, 240, 1536, 512], P(None, 'lat', 'lon'), may hold values from -16 to 16
- land_sea: int32 [2, 240, 1536], P(None, 'lat', 'lon'), may hold values from 0 to 2
- w_qkv: bfloat16 [512, 1536], replicated, may hold values from -0.25 to 0.25
- w_out: bfloat16 [512, 512], replicated, may hold values from -0.25 to 0.25
- norm_gain: float32 [512], replicated, may hold values from 0.1 to 1.9
Outputs:
- mixed: bfloat16 [2, 240, 1536, 512], P(None, 'lat', 'lon')
The draws below stay inside these ranges and needn't reach their ends.
All inputs are finite; a program needn't handle non-finite values.
Results may differ from the reference program's by a relative error of at most 0.006.
Values may be sent and summed in bfloat16 or wider, within the bound.
A program may use at most 192 MiB of HBM per device.

```python
import jax
import jax.numpy as jnp
from jax import lax

D = 512
HEADS = 8
HEAD = 64
LEVELS = 2
WIN_LAT = 6
WIN_LON = 12
NLAT = 240
NLON = 1536


def draw_tokens(key, part):
    key = jax.random.fold_in(key, 11)
    first = jax.random.fold_in(key, 0)
    base = jax.random.normal(first, (LEVELS, NLAT, NLON, D), jnp.float32)
    return jnp.clip(base, -16.0, 16.0).astype(jnp.bfloat16)


def set_ends(array, stream_key, least, high):
    shape = array.shape
    index_at = [jax.random.randint(jax.random.fold_in(stream_key, axis), (), 0, shape[axis]) for axis in range(len(shape))]
    array = array.at[tuple(index_at)].set(least)
    longest = shape.index(max(shape))
    index_at[longest] = (index_at[longest] + 1) % shape[longest]
    return array.at[tuple(index_at)].set(high)


def centred(key, shape, scale, reach, held_as=jnp.bfloat16):
    values = jax.random.normal(key, shape, jnp.float32) * scale
    return jnp.minimum(jnp.maximum(values, -reach), reach).astype(held_as)


def setup_inputs(seed: int = 0) -> dict:
    seeds = jax.random.split(jax.random.key(seed), 6)
    return {
        "tokens": draw_tokens(jax.random.fold_in(seeds[5], 71), 0),
        "land_sea": set_ends(jax.random.randint(seeds[1], (LEVELS, NLAT, NLON), 0, 3), jax.random.fold_in(seeds[1], 1), 0, 2).astype(jnp.int32),
        "w_qkv": centred(seeds[2], (D, 3 * D), D ** -0.5, 0.25),
        "w_out": centred(seeds[3], (D, D), D ** -0.5, 0.25),
        "norm_gain": jnp.clip(1.0 + 0.18 * jax.random.normal(seeds[4], (D,), jnp.float32), 0.1, 1.9),
    }


def to_windows(t):
    lev, rows, cols = (t.shape[0], t.shape[1], t.shape[2])
    rest = t.shape[3:]
    t = t.reshape((lev, rows // WIN_LAT, WIN_LAT, cols // WIN_LON, WIN_LON) + rest)
    order = (1, 3, 0, 2, 4) + tuple(range(5, 5 + len(rest)))
    t = jnp.transpose(t, order)
    return t.reshape((rows // WIN_LAT * (cols // WIN_LON), lev * WIN_LAT * WIN_LON) + rest)

def from_windows(t, lev, rows, cols):
    rest = t.shape[2:]
    t = t.reshape((rows // WIN_LAT, cols // WIN_LON, lev, WIN_LAT, WIN_LON) + rest)
    order = (2, 0, 3, 1, 4) + tuple(range(5, 5 + len(rest)))
    return jnp.transpose(t, order).reshape((lev, rows, cols) + rest)

def attend(block, surface, edge_rows, w_qkv, w_out, norm_gain):
    lev, rows, cols, width = block.shape
    qkv = jnp.dot(block.reshape(-1, width), w_qkv, preferred_element_type=jnp.float32).astype(jnp.bfloat16)
    qkv = to_windows(qkv.reshape(lev, rows, cols, 3 * width))
    count = qkv.shape[1]
    query = qkv[:, :, :width].reshape(-1, count, HEADS, HEAD).astype(jnp.float32)
    keys = qkv[:, :, width:2 * width].reshape(-1, count, HEADS, HEAD).astype(jnp.float32)
    values = qkv[:, :, 2 * width:].reshape(-1, count, HEADS, HEAD).astype(jnp.float32)
    group = surface * 2 + jnp.broadcast_to(edge_rows[None, :, None], surface.shape)
    group = to_windows(group)
    allowed = group[:, None, :, None] == group[:, None, None, :]
    scores = jnp.einsum('wqhd,wkhd->whqk', query, keys) * (1.0 / HEAD ** 0.5)
    masked = jnp.where(allowed, scores, -jnp.inf)
    top = lax.optimization_barrier(jnp.max(masked, axis=-1, keepdims=True))
    expo = jnp.where(allowed, jnp.exp(masked - top), 0.0)
    probs = (expo / lax.optimization_barrier(jnp.sum(expo, axis=-1, keepdims=True))).astype(jnp.bfloat16)
    att = jnp.einsum('whqk,wkhd->wqhd', probs.astype(jnp.float32), values).astype(jnp.bfloat16)
    att = from_windows(att.reshape(-1, count, width), lev, rows, cols)
    proj = jnp.dot(att.reshape(-1, width), w_out, preferred_element_type=jnp.float32)
    centre = proj - lax.optimization_barrier(jnp.mean(proj, axis=-1, keepdims=True))
    spread = lax.optimization_barrier(jnp.mean(centre * centre, axis=-1, keepdims=True))
    normed = norm_gain * centre / jnp.sqrt(spread + 1e-05)
    result = block.reshape(-1, width).astype(jnp.float32) + normed
    return result.astype(jnp.bfloat16).reshape(lev, rows, cols, width)

def reference(tokens, land_sea, w_qkv, w_out, norm_gain):
    shifted = jnp.roll(tokens, (-(WIN_LAT // 2), -(WIN_LON // 2)), axis=(1, 2))
    edge = (jnp.arange(NLAT) >= NLAT - WIN_LAT // 2).astype(jnp.int32)
    bands = NLAT // WIN_LAT
    blocks = jnp.transpose(shifted.reshape(LEVELS, bands, WIN_LAT, NLON, D), (1, 0, 2, 3, 4))
    surf = jnp.transpose(land_sea.reshape(LEVELS, bands, WIN_LAT, NLON), (1, 0, 2, 3))
    edges = edge.reshape(bands, WIN_LAT)

    def one_band(items):
        return attend(items[0], items[1], items[2], w_qkv, w_out, norm_gain)
    out = lax.map(one_band, (blocks, surf, edges))
    out = jnp.transpose(out, (1, 0, 2, 3, 4)).reshape(LEVELS, NLAT, NLON, D)
    return jnp.roll(out, (WIN_LAT // 2, WIN_LON // 2), axis=(1, 2))
```

```python
import functools

import jax
import jax.numpy as jnp
import numpy as np
from jax import lax
from jax.experimental import pallas as pl
from jax.experimental.pallas import tpu as pltpu
from jax.sharding import PartitionSpec as P

HEADS = 8
HEAD = 64
WIN_LAT = 6
WIN_LON = 12
HALF_LAT = 3
HALF_LON = 6
LEV = 2
COLS = 24
D = 512
STEPS = 10
COMBOS = LEV * WIN_LAT
COUNT = COMBOS * WIN_LON
EDGE = COMBOS * HALF_LON
START = 5
AHEAD = 3
BIG = 1e30
MESH = pl.DeviceIdType.MESH
F32 = jnp.float32
BF16 = jnp.bfloat16


def centre_tokens():
    found = [(n, 8 + s) for n in range(COMBOS) for s in range(8)]
    for m in range(COMBOS // 2):
        found += [(2 * m, 16), (2 * m, 17), (2 * m + 1, 16), (2 * m + 1, 17)]
        found += [(2 * m + 1, 6), (2 * m + 1, 7), (2 * m, 6), (2 * m, 7)]
    return found


def left_tokens():
    found = []
    for n in range(9):
        k = n % 3
        found += [(n, s) for s in range(6)] + [(9 + n // 3, 2 * k), (9 + n // 3, 2 * k + 1)]
    return found


def right_tokens():
    found = []
    for n in range(9):
        k = n % 3
        found += [(9 + n // 3, 18 + 2 * k), (9 + n // 3, 19 + 2 * k)] + [(n, 16 + s) for s in range(2, 8)]
    return found


def tables():
    split = [(n, c - HALF_LON) for n, c in right_tokens()] + [(n, c + 18) for n, c in left_tokens()]
    both = [(n, c - HALF_LON) for n, c in centre_tokens()] + split
    column = np.zeros((2 * COUNT, 32), np.float32)
    lane = np.zeros((2 * COUNT, 128), np.int32)
    lower = np.zeros((2 * COUNT, 128), np.float32)
    for t, (n, c) in enumerate(both):
        level, row = divmod(n, WIN_LAT)
        column[t, c] = 1.0
        lane[t] = np.arange(128) - (64 * level + row)
        lower[t] = 3.0 if row >= HALF_LAT else 0.0
    return column.astype(jnp.bfloat16), lane, lower


def dot(a, b):
    return lax.dot_general(a, b, (((1,), (0,)), ((), ())), preferred_element_type=F32)


def dot_t(a, b):
    return lax.dot_general(a, b, (((1,), (1,)), ((), ())), preferred_element_type=F32)


def rows_of(shape):
    return lax.broadcasted_iota(jnp.int32, shape, 0)


def lanes_of(shape):
    return lax.broadcasted_iota(jnp.int32, shape, 1)


def roll(x, by):
    return pltpu.roll(x, by, 0)


def attend(q, hot, k, far, v):
    n = q.shape[0]
    first = lanes_of((n, 128)) < HEAD
    hot2 = jnp.concatenate([hot, hot], axis=0).astype(BF16)
    ones = jnp.ones((COUNT, 128), BF16)
    found = []
    for pair in range(HEADS // 2):
        cut = slice(128 * pair, 128 * pair + 128)
        part = q[:, cut] * (1.0 / HEAD**0.5)
        q2 = jnp.concatenate([jnp.where(first, part, 0.0), jnp.where(first, 0.0, part)], axis=0).astype(BF16)
        scores = dot_t(jnp.concatenate([q2, hot2], axis=1), jnp.concatenate([k[:, cut], far], axis=1))
        top = jnp.max(scores, axis=1, keepdims=True)
        expo = jnp.exp(scores - top).astype(BF16)
        summed = dot(expo, jnp.concatenate([v[:, cut], ones], axis=1))
        probs = summed[:, :128] / summed[:, 128:]
        found.append(jnp.where(first, probs[:n], probs[n:]))
    return jnp.concatenate(found, axis=1)


def finish(x, att, w_out, gain):
    proj = dot(att.astype(BF16), w_out)
    centre = proj - jnp.mean(proj, axis=1, keepdims=True)
    spread = jnp.mean(centre * centre, axis=1, keepdims=True)
    return x + gain * (centre * lax.rsqrt(spread + 1e-05))


def features(spread, lane, lower, step, edge):
    surface = jnp.sum(jnp.where(lane == WIN_LAT * step, spread, 0.0), axis=1, keepdims=True)
    same = surface + lower * edge == lanes_of((COUNT, 128)).astype(F32)
    return jnp.where(same, 1.0, 0.0), jnp.where(same, 0.0, -BIG).astype(BF16)


def fold(x):
    return jnp.concatenate([x[:, : D // 2], x[:, D // 2 :]], axis=0).astype(BF16)


def unfold(x):
    x = x.astype(F32)
    return jnp.concatenate([x[:EDGE], x[EDGE:]], axis=1)


def kernel(
    tokens, land, w_qkv, w_out, gain, column, lane, lower, out,
    xs, land_v, wq_v, wo_v, gain_v, column_v, lane_v, lower_v,
    to_west, to_east, from_west, from_east, mine, theirs, spread, centre, res,
    x_sem, x9_sem, in_sem, lat_sem, land_sem, west_send, west_recv, east_send, east_recv, out_sem, back_sem,
):
    lon, lat = lax.axis_index("lon"), lax.axis_index("lat")
    nlon, nlat = lax.axis_size("lon"), lax.axis_size("lat")
    west = (lax.rem(lon + nlon - 1, nlon), lat)
    east = (lax.rem(lon + 1, nlon), lat)
    north = (lon, lax.rem(lat + nlat - 1, nlat))
    south = (lon, lax.rem(lat + 1, nlat))
    last = jnp.where(lat == nlat - 1, 1.0, 0.0)

    barrier = pltpu.get_barrier_semaphore()
    for near in (west, east, north, south):
        pl.semaphore_signal(barrier, inc=1, device_id=near, device_id_type=MESH)

    def x_copy(a):
        return pltpu.make_async_copy(tokens.at[:, pl.ds(WIN_LAT * a + HALF_LAT, WIN_LAT)], xs.at[a], x_sem.at[a])

    x9_copy = pltpu.make_async_copy(
        tokens.at[:, WIN_LAT * STEPS - HALF_LAT : WIN_LAT * STEPS], xs.at[STEPS - 1, :, 0:HALF_LAT], x9_sem
    )
    ins = [
        pltpu.make_async_copy(src, dst, in_sem.at[i])
        for i, (src, dst) in enumerate(
            [(land, land_v), (column, column_v), (lane, lane_v), (lower, lower_v), (gain, gain_v), (w_qkv, wq_v), (w_out, wo_v)]
        )
    ]

    def remote(src, dst, send, recv, device):
        return pltpu.make_async_remote_copy(
            src_ref=src, dst_ref=dst, send_sem=send, recv_sem=recv, device_id=device, device_id_type=MESH
        )

    lat_copy = remote(tokens.at[:, 0:HALF_LAT], xs.at[STEPS - 1, :, HALF_LAT:WIN_LAT], lat_sem.at[0], lat_sem.at[1], north)
    land_copy = remote(mine, theirs, land_sem.at[0], land_sem.at[1], east)
    back_copy = remote(res.at[STEPS - 1, :, HALF_LAT:WIN_LAT], out.at[:, 0:HALF_LAT], back_sem.at[0], back_sem.at[1], south)

    def west_copy(a):
        return remote(to_west.at[a], from_east.at[a], west_send.at[a], west_recv.at[a], west)

    def east_copy(a):
        return remote(to_east.at[a], from_west.at[a], east_send.at[a], east_recv.at[a], east)

    def out_copy(a):
        return pltpu.make_async_copy(res.at[a], out.at[:, pl.ds(WIN_LAT * a + HALF_LAT, WIN_LAT)], out_sem.at[a])

    out9_copy = pltpu.make_async_copy(
        res.at[STEPS - 1, :, 0:HALF_LAT], out.at[:, WIN_LAT * STEPS - HALF_LAT : WIN_LAT * STEPS], out_sem.at[STEPS - 1]
    )

    for i in range(STEPS):
        a = (i + START) % STEPS
        if a == STEPS - 1:
            x9_copy.start()
        else:
            x_copy(a).start()
        if i == 0:
            for copy in ins:
                copy.start()
    pl.semaphore_wait(barrier, 4)
    lat_copy.start()

    row8 = rows_of((8, D))

    def tile(a, n, c):
        return xs[a, n // WIN_LAT, n % WIN_LAT, 8 * c : 8 * c + 8, :].astype(F32)

    def send(a):
        t0 = [tile(a, n, 0) for n in range(COMBOS)]
        t2 = [tile(a, n, 2) for n in range(COMBOS)]
        left = [jnp.where(row8 < 6, t0[n], roll(t0[9 + n // 3], 6 - 2 * (n % 3))) for n in range(9)]
        right = [jnp.where(row8 >= 2, t2[n], roll(t2[9 + n // 3], 6 - 2 * (n % 3))) for n in range(9)]
        to_west[a] = fold(jnp.concatenate(left, axis=0))
        to_east[a] = fold(jnp.concatenate(right, axis=0))
        west_copy(a).start()
        east_copy(a).start()

    def whole(a):
        t0 = [tile(a, n, 0) for n in range(COMBOS)]
        t2 = [tile(a, n, 2) for n in range(COMBOS)]
        parts = [tile(a, n, 1) for n in range(COMBOS)]
        for m in range(COMBOS // 2):
            low = jnp.where(row8 < 2, t2[2 * m], roll(t2[2 * m + 1], 2))
            high = jnp.where(row8 < 6, roll(t0[2 * m + 1], 6), t0[2 * m])
            parts.append(jnp.where(row8 < 4, low, high))
        x = jnp.concatenate(parts, axis=0)
        qkv = dot(x.astype(BF16), wq_v[...])
        edge = last * jnp.where(a == STEPS - 1, 1.0, 0.0)
        hot, far = features(spread[0], lane_v[:COUNT], lower_v[:COUNT], a, edge)
        att = attend(qkv[:, :D], hot, qkv[:, D : 2 * D].astype(BF16), far, qkv[:, 2 * D :].astype(BF16))
        centre[a] = finish(x, att, wo_v[...], gain_v[...]).astype(BF16)

    def split(a):
        left, right = unfold(to_west[a]), unfold(to_east[a])
        before = jnp.concatenate([unfold(from_west[a]), left], axis=0).astype(BF16)
        after = jnp.concatenate([right, unfold(from_east[a])], axis=0).astype(BF16)
        x = jnp.concatenate([left, right], axis=0)
        q = dot(x.astype(BF16), wq_v[:, :D])
        kv = dot(jnp.concatenate([before, after], axis=0), wq_v[:, D:]).astype(BF16)
        edge = last * jnp.where(a == STEPS - 1, 1.0, 0.0)
        lanes, lowers = lane_v[COUNT:], lower_v[COUNT:]
        hot0, far0 = features(spread[1], lanes, lowers, a, edge)
        hot2, far2 = features(spread[2], lanes, lowers, a, edge)
        att0 = attend(q[:EDGE], hot0[EDGE:], kv[:COUNT, :D], far0, kv[:COUNT, D:])
        att2 = attend(q[EDGE:], hot2[:EDGE], kv[COUNT:, :D], far2, kv[COUNT:, D:])
        y = finish(x, jnp.concatenate([att0, att2], axis=0), wo_v[...], gain_v[...])
        lefts = [y[8 * n : 8 * n + 8] for n in range(9)]
        rights = [y[EDGE + 8 * n : EDGE + 8 * n + 8] for n in range(9)]
        mid = centre[a].astype(F32)
        for n in range(COMBOS):
            rest = mid[96 + 8 * (n // 2) : 104 + 8 * (n // 2)]
            rest0, rest2 = (rest, rest) if n % 2 == 0 else (roll(rest, 2), roll(rest, 6))
            if n < 9:
                tile0 = jnp.where(row8 < 6, lefts[n], rest0)
                tile2 = jnp.where(row8 >= 2, rights[n], rest2)
            else:
                b = 3 * (n - 9)
                low = jnp.where(row8 < 2, roll(lefts[b], 2), roll(lefts[b + 1], 4))
                tile0 = jnp.where(row8 < 4, low, jnp.where(row8 < 6, roll(lefts[b + 2], 6), rest0))
                low = jnp.where(row8 < 2, rest2, roll(rights[b], 2))
                tile2 = jnp.where(row8 < 4, low, jnp.where(row8 < 6, roll(rights[b + 1], 4), roll(rights[b + 2], 6)))
            whole_row = jnp.concatenate([tile0, mid[8 * n : 8 * n + 8], tile2], axis=0)
            res[a, n // WIN_LAT, n % WIN_LAT] = whole_row.astype(BF16)

    def early(i, carry):
        a = i + START
        x_copy(a).wait()
        send(a)
        return carry

    lax.fori_loop(0, STEPS - 1 - START, early, 0)

    for copy in ins[:4]:
        copy.wait()
    across = jnp.zeros((COLS, 128), F32)
    rows = land_v.shape[2]
    for level in range(LEV):
        place = rows_of((rows, 128)) + 64 * level == lanes_of((rows, 128))
        across += dot(land_v[level].astype(F32).astype(BF16), jnp.where(place, 1.0, 0.0).astype(BF16))
    mine[...] = jnp.concatenate([across, jnp.zeros((32 - COLS, 128), F32)], axis=0).astype(BF16)
    land_copy.start()
    spread[0] = dot(column_v[:COUNT], mine[...])
    spread[2] = dot(column_v[COUNT:], mine[...])
    for copy in ins[4:]:
        copy.wait()

    def ahead(i, carry):
        whole(i + START)
        return carry

    lax.fori_loop(0, AHEAD, ahead, 0)
    x9_copy.wait()
    lat_copy.wait()
    send(STEPS - 1)

    def late(a, carry):
        x_copy(a).wait()
        send(a)
        return carry

    lax.fori_loop(0, START, late, 0)
    land_copy.wait()
    spread[1] = dot(column_v[COUNT:], theirs[...])

    def step(i, carry):
        a = lax.rem(i + START, STEPS)
        west_copy(a).wait()
        east_copy(a).wait()
        split(a)

        @pl.when(a == STEPS - 1)
        def _():
            back_copy.start()
            out9_copy.start()

        @pl.when(a != STEPS - 1)
        def _():
            out_copy(a).start()

        @pl.when(i < STEPS - AHEAD)
        def _():
            whole(lax.rem(i + AHEAD + START, STEPS))

        return carry

    lax.fori_loop(0, STEPS, step, 0)

    def drain(a, carry):
        out_copy(a).wait()
        return carry

    lax.fori_loop(0, STEPS - 1, drain, 0)
    out9_copy.wait()
    back_copy.wait()


def body(tokens, land_sea, w_qkv, w_out, norm_gain):
    column, lane, lower = tables()
    land_sea = jnp.transpose(land_sea, (0, 2, 1))
    anywhere = pl.BlockSpec(memory_space=pl.ANY)
    hbm = pl.BlockSpec(memory_space=pltpu.HBM)
    dma = pltpu.SemaphoreType.DMA
    vmem = pltpu.VMEM
    band = (STEPS, LEV, WIN_LAT, COLS, D)
    folded = (STEPS, COUNT, D // 2)
    return pl.pallas_call(
        kernel,
        out_shape=jax.ShapeDtypeStruct(tokens.shape, BF16),
        in_specs=[hbm] * 8,
        out_specs=anywhere,
        scratch_shapes=[
            vmem(band, BF16),
            vmem(land_sea.shape, jnp.int32),
            vmem(w_qkv.shape, BF16),
            vmem(w_out.shape, BF16),
            vmem((1, D), F32),
            vmem(column.shape, BF16),
            vmem(lane.shape, jnp.int32),
            vmem(lower.shape, F32),
            vmem(folded, BF16),
            vmem(folded, BF16),
            vmem(folded, BF16),
            vmem(folded, BF16),
            vmem((32, 128), BF16),
            vmem((32, 128), BF16),
            vmem((3, COUNT, 128), F32),
            vmem((STEPS, COUNT, D), BF16),
            vmem(band, BF16),
            dma((STEPS,)),
            dma,
            dma((7,)),
            dma((2,)),
            dma((2,)),
            dma((STEPS,)),
            dma((STEPS,)),
            dma((STEPS,)),
            dma((STEPS,)),
            dma((STEPS,)),
            dma((2,)),
        ],
        compiler_params=pltpu.CompilerParams(
            collective_id=0, has_side_effects=True, vmem_limit_bytes=63 * 1024 * 1024
        ),
    )(tokens, land_sea, w_qkv, w_out, norm_gain.reshape(1, D), column, lane, lower)


def solution(mesh):
    in_specs = (P(None, "lat", "lon", None), P(None, "lat", "lon"), P(), P(), P())
    out_specs = P(None, "lat", "lon", None)
    return jax.shard_map(body, mesh=mesh, in_specs=in_specs, out_specs=out_specs, check_vma=False)
```

```python
import functools

import jax
import jax.numpy as jnp
import numpy as np
from jax import lax
from jax.experimental import pallas as pl
from jax.experimental.pallas import tpu as pltpu
from jax.sharding import PartitionSpec as P

HEADS = 8
HEAD = 64
WIN_LAT = 6
WIN_LON = 12
HALF_LAT = 3
HALF_LON = 6
LEV = 2
COLS = 24
D = 512
STEPS = 10
COMBOS = LEV * WIN_LAT
COUNT = COMBOS * WIN_LON
EDGE = COMBOS * HALF_LON
START = 2
AHEAD = 3
BIG = 1e30
MESH = pl.DeviceIdType.MESH
F32 = jnp.float32
BF16 = jnp.bfloat16


def centre_tokens():
    found = [(n, 8 + s) for n in range(COMBOS) for s in range(8)]
    for m in range(COMBOS // 2):
        found += [(2 * m, 16), (2 * m, 17), (2 * m + 1, 16), (2 * m + 1, 17)]
        found += [(2 * m + 1, 6), (2 * m + 1, 7), (2 * m, 6), (2 * m, 7)]
    return found


def left_tokens():
    found = []
    for n in range(9):
        k = n % 3
        found += [(n, s) for s in range(6)] + [(9 + n // 3, 2 * k), (9 + n // 3, 2 * k + 1)]
    return found


def right_tokens():
    found = []
    for n in range(9):
        k = n % 3
        found += [(9 + n // 3, 18 + 2 * k), (9 + n // 3, 19 + 2 * k)] + [(n, 16 + s) for s in range(2, 8)]
    return found


def tables():
    split = [(n, c - HALF_LON) for n, c in right_tokens()] + [(n, c + 18) for n, c in left_tokens()]
    both = [(n, c - HALF_LON) for n, c in centre_tokens()] + split
    column = np.zeros((2 * COUNT, 32), np.float32)
    lane = np.zeros((2 * COUNT, 128), np.int32)
    lower = np.zeros((2 * COUNT, 128), np.float32)
    for t, (n, c) in enumerate(both):
        level, row = divmod(n, WIN_LAT)
        column[t, c] = 1.0
        lane[t] = np.arange(128) - (64 * level + row)
        lower[t] = 3.0 if row >= HALF_LAT else 0.0
    return column.astype(jnp.bfloat16), lane, lower


def dot(a, b):
    return lax.dot_general(a, b, (((1,), (0,)), ((), ())), preferred_element_type=F32)


def dot_t(a, b):
    return lax.dot_general(a, b, (((1,), (1,)), ((), ())), preferred_element_type=F32)


def rows_of(shape):
    return lax.broadcasted_iota(jnp.int32, shape, 0)


def lanes_of(shape):
    return lax.broadcasted_iota(jnp.int32, shape, 1)


def roll(x, by):
    return pltpu.roll(x, by, 0)


def attend(q, hot, k, far, v):
    n = q.shape[0]
    first = lanes_of((n, 128)) < HEAD
    keep0 = jnp.where(lanes_of((1, 128)) < HEAD, 1.0 / HEAD**0.5, 0.0)
    keep1 = jnp.where(lanes_of((1, 128)) < HEAD, 0.0, 1.0 / HEAD**0.5)
    hot2 = jnp.concatenate([hot, hot], axis=0).astype(BF16)
    ones = jnp.ones((COUNT, 128), BF16)
    found = []
    for pair in range(HEADS // 2):
        cut = slice(128 * pair, 128 * pair + 128)
        part = q[:, cut]
        q2 = jnp.concatenate([part * keep0, part * keep1], axis=0).astype(BF16)
        scores = dot_t(jnp.concatenate([q2, hot2], axis=1), jnp.concatenate([k[:, cut], far], axis=1))
        top = jnp.max(scores, axis=1, keepdims=True)
        expo = jnp.exp(scores - top).astype(BF16)
        summed = dot(expo, jnp.concatenate([v[:, cut], ones], axis=1))
        top_part = jnp.where(first, summed[:n, :128], summed[n:, :128])
        found.append(top_part / jnp.where(first, summed[:n, 128:], summed[n:, 128:]))
    return jnp.concatenate(found, axis=1)


def finish(x, att, w_out, gain):
    proj = dot(att.astype(BF16), w_out)
    centre = proj - jnp.mean(proj, axis=1, keepdims=True)
    spread = jnp.mean(centre * centre, axis=1, keepdims=True)
    return x + gain * (centre * lax.rsqrt(spread + 1e-05))


def features(spread, lane, lower, step, edge):
    surface = jnp.sum(jnp.where(lane == WIN_LAT * step, spread, 0.0), axis=1, keepdims=True)
    same = surface + lower * edge == lanes_of((COUNT, 128)).astype(F32)
    return jnp.where(same, 1.0, 0.0), jnp.where(same, 0.0, -BIG).astype(BF16)


def fold(x):
    return jnp.concatenate([x[:, : D // 2], x[:, D // 2 :]], axis=0).astype(BF16)


def unfold(x):
    x = x.astype(F32)
    return jnp.concatenate([x[:EDGE], x[EDGE:]], axis=1)


def kernel(
    tokens, land, w_qkv, w_out, gain, column, lane, lower, out,
    xs, land_v, wq_v, wo_v, gain_v, column_v, lane_v, lower_v,
    to_west, to_east, from_west, from_east, mine, theirs, spread, centre, res,
    x_sem, x9_sem, in_sem, lat_sem, land_sem, west_send, west_recv, east_send, east_recv, out_sem, back_sem,
):
    lon, lat = lax.axis_index("lon"), lax.axis_index("lat")
    nlon, nlat = lax.axis_size("lon"), lax.axis_size("lat")
    west = (lax.rem(lon + nlon - 1, nlon), lat)
    east = (lax.rem(lon + 1, nlon), lat)
    north = (lon, lax.rem(lat + nlat - 1, nlat))
    south = (lon, lax.rem(lat + 1, nlat))
    last = jnp.where(lat == nlat - 1, 1.0, 0.0)

    barrier = pltpu.get_barrier_semaphore()
    for near in (west, east, north, south):
        pl.semaphore_signal(barrier, inc=1, device_id=near, device_id_type=MESH)

    def x_copy(a):
        return pltpu.make_async_copy(tokens.at[:, pl.ds(WIN_LAT * a + HALF_LAT, WIN_LAT)], xs.at[a], x_sem.at[a])

    x9_copy = pltpu.make_async_copy(
        tokens.at[:, WIN_LAT * STEPS - HALF_LAT : WIN_LAT * STEPS], xs.at[STEPS - 1, :, 0:HALF_LAT], x9_sem
    )
    ins = [
        pltpu.make_async_copy(src, dst, in_sem.at[i])
        for i, (src, dst) in enumerate(
            [(land, land_v), (column, column_v), (lane, lane_v), (lower, lower_v), (gain, gain_v), (w_qkv, wq_v), (w_out, wo_v)]
        )
    ]

    def remote(src, dst, send, recv, device):
        return pltpu.make_async_remote_copy(
            src_ref=src, dst_ref=dst, send_sem=send, recv_sem=recv, device_id=device, device_id_type=MESH
        )

    lat_copy = remote(tokens.at[:, 0:HALF_LAT], xs.at[STEPS - 1, :, HALF_LAT:WIN_LAT], lat_sem.at[0], lat_sem.at[1], north)
    land_copy = remote(mine, theirs, land_sem.at[0], land_sem.at[1], east)
    back_copy = remote(res.at[STEPS - 1, :, HALF_LAT:WIN_LAT], out.at[:, 0:HALF_LAT], back_sem.at[0], back_sem.at[1], south)

    def west_copy(a):
        return remote(to_west.at[a], from_east.at[a], west_send.at[a], west_recv.at[a], west)

    def east_copy(a):
        return remote(to_east.at[a], from_west.at[a], east_send.at[a], east_recv.at[a], east)

    def out_copy(a):
        return pltpu.make_async_copy(res.at[a], out.at[:, pl.ds(WIN_LAT * a + HALF_LAT, WIN_LAT)], out_sem.at[a])

    out9_copy = pltpu.make_async_copy(
        res.at[STEPS - 1, :, 0:HALF_LAT], out.at[:, WIN_LAT * STEPS - HALF_LAT : WIN_LAT * STEPS], out_sem.at[STEPS - 1]
    )

    for i in range(STEPS):
        a = (i + START) % STEPS
        if a == STEPS - 1:
            x9_copy.start()
        else:
            x_copy(a).start()
        if i == 0:
            for copy in ins:
                copy.start()
    pl.semaphore_wait(barrier, 4)
    lat_copy.start()

    row8 = rows_of((8, D))

    def tile(a, n, c):
        return xs[a, n // WIN_LAT, n % WIN_LAT, 8 * c : 8 * c + 8, :].astype(F32)

    def send(a):
        t0 = [tile(a, n, 0) for n in range(COMBOS)]
        t2 = [tile(a, n, 2) for n in range(COMBOS)]
        left = [jnp.where(row8 < 6, t0[n], roll(t0[9 + n // 3], 6 - 2 * (n % 3))) for n in range(9)]
        right = [jnp.where(row8 >= 2, t2[n], roll(t2[9 + n // 3], 6 - 2 * (n % 3))) for n in range(9)]
        to_west[a] = fold(jnp.concatenate(left, axis=0))
        to_east[a] = fold(jnp.concatenate(right, axis=0))
        west_copy(a).start()
        east_copy(a).start()

    def whole(a):
        t0 = [tile(a, n, 0) for n in range(COMBOS)]
        t2 = [tile(a, n, 2) for n in range(COMBOS)]
        parts = [tile(a, n, 1) for n in range(COMBOS)]
        for m in range(COMBOS // 2):
            low = jnp.where(row8 < 2, t2[2 * m], roll(t2[2 * m + 1], 2))
            high = jnp.where(row8 < 6, roll(t0[2 * m + 1], 6), t0[2 * m])
            parts.append(jnp.where(row8 < 4, low, high))
        x = jnp.concatenate(parts, axis=0)
        qkv = dot(x.astype(BF16), wq_v[...])
        edge = last * jnp.where(a == STEPS - 1, 1.0, 0.0)
        hot, far = features(spread[0], lane_v[:COUNT], lower_v[:COUNT], a, edge)
        att = attend(qkv[:, :D], hot, qkv[:, D : 2 * D].astype(BF16), far, qkv[:, 2 * D :].astype(BF16))
        centre[a] = finish(x, att, wo_v[...], gain_v[...]).astype(BF16)

    def split(a):
        left, right = unfold(to_west[a]), unfold(to_east[a])
        before = jnp.concatenate([unfold(from_west[a]), left], axis=0).astype(BF16)
        after = jnp.concatenate([right, unfold(from_east[a])], axis=0).astype(BF16)
        x = jnp.concatenate([left, right], axis=0)
        q = dot(x.astype(BF16), wq_v[:, :D])
        kv = dot(jnp.concatenate([before, after], axis=0), wq_v[:, D:]).astype(BF16)
        edge = last * jnp.where(a == STEPS - 1, 1.0, 0.0)
        lanes, lowers = lane_v[COUNT:], lower_v[COUNT:]
        hot0, far0 = features(spread[1], lanes, lowers, a, edge)
        hot2, far2 = features(spread[2], lanes, lowers, a, edge)
        att0 = attend(q[:EDGE], hot0[EDGE:], kv[:COUNT, :D], far0, kv[:COUNT, D:])
        att2 = attend(q[EDGE:], hot2[:EDGE], kv[COUNT:, :D], far2, kv[COUNT:, D:])
        y = finish(x, jnp.concatenate([att0, att2], axis=0), wo_v[...], gain_v[...])
        lefts = [y[8 * n : 8 * n + 8] for n in range(9)]
        rights = [y[EDGE + 8 * n : EDGE + 8 * n + 8] for n in range(9)]
        mid = centre[a].astype(F32)
        for n in range(COMBOS):
            rest = mid[96 + 8 * (n // 2) : 104 + 8 * (n // 2)]
            rest0, rest2 = (rest, rest) if n % 2 == 0 else (roll(rest, 2), roll(rest, 6))
            if n < 9:
                tile0 = jnp.where(row8 < 6, lefts[n], rest0)
                tile2 = jnp.where(row8 >= 2, rights[n], rest2)
            else:
                b = 3 * (n - 9)
                low = jnp.where(row8 < 2, roll(lefts[b], 2), roll(lefts[b + 1], 4))
                tile0 = jnp.where(row8 < 4, low, jnp.where(row8 < 6, roll(lefts[b + 2], 6), rest0))
                low = jnp.where(row8 < 2, rest2, roll(rights[b], 2))
                tile2 = jnp.where(row8 < 4, low, jnp.where(row8 < 6, roll(rights[b + 1], 4), roll(rights[b + 2], 6)))
            whole_row = jnp.concatenate([tile0, mid[8 * n : 8 * n + 8], tile2], axis=0)
            res[a, n // WIN_LAT, n % WIN_LAT] = whole_row.astype(BF16)

    def both(a, b):
        split(a)
        whole(b)

    nine = STEPS - 1 - START

    nine = STEPS - 1 - START
    calm = lon == nlon - 1

    def early(i):
        send(lax.rem(i + START, STEPS - 1))

    x_copy(START).wait()
    early(0)

    def loaded(i, carry):
        x_copy(lax.rem(i + START, STEPS - 1)).wait()
        return carry

    lax.fori_loop(1, STEPS - 1, loaded, 0)

    for copy in ins[:4]:
        copy.wait()
    across = jnp.zeros((COLS, 128), F32)
    rows = land_v.shape[2]
    for level in range(LEV):
        place = rows_of((rows, 128)) + 64 * level == lanes_of((rows, 128))
        across += dot(land_v[level].astype(F32).astype(BF16), jnp.where(place, 1.0, 0.0).astype(BF16))
    mine[...] = jnp.concatenate([across, jnp.zeros((32 - COLS, 128), F32)], axis=0).astype(BF16)
    land_copy.start()
    spread[0] = dot(column_v[:COUNT], mine[...])
    spread[2] = dot(column_v[COUNT:], mine[...])
    for copy in ins[4:]:
        copy.wait()

    def ahead(i, carry):
        whole(i + START)

        @pl.when(((i == 0) & ~calm) | ((i == 1) & calm))
        def _():
            early(1)

        @pl.when((i == 2) & ~calm)
        def _():
            early(2)

        return carry

    lax.fori_loop(0, AHEAD, ahead, 0)
    land_copy.wait()
    spread[1] = dot(column_v[COUNT:], theirs[...])

    def step(i, carry, more):
        a = lax.rem(i + START, STEPS)
        if more:
            @pl.when((i < nine - AHEAD) & ~calm)
            def _():
                early(i + AHEAD)

            @pl.when((i > nine - AHEAD) | calm)
            def _():
                early(i + AHEAD - 1)

            @pl.when(i == nine - AHEAD)
            def _():
                x9_copy.wait()
                lat_copy.wait()
                send(STEPS - 1)

        west_copy(a).wait()
        east_copy(a).wait()
        if more:
            both(a, lax.rem(i + AHEAD + START, STEPS))
        else:
            split(a)

        @pl.when(a == STEPS - 1)
        def _():
            back_copy.start()
            out9_copy.start()

        @pl.when(a != STEPS - 1)
        def _():
            out_copy(a).start()

        return carry

    lax.fori_loop(0, STEPS - AHEAD, functools.partial(step, more=True), 0)
    lax.fori_loop(STEPS - AHEAD, STEPS, functools.partial(step, more=False), 0)

    def drain(a, carry):
        out_copy(a).wait()
        return carry

    lax.fori_loop(0, STEPS - 1, drain, 0)
    out9_copy.wait()
    back_copy.wait()


def body(tokens, land_sea, w_qkv, w_out, norm_gain):
    column, lane, lower = tables()
    land_sea = jnp.transpose(land_sea, (0, 2, 1))
    anywhere = pl.BlockSpec(memory_space=pl.ANY)
    operands = (tokens, land_sea, w_qkv, w_out, norm_gain.reshape(1, D), column, lane, lower)
    dma = pltpu.SemaphoreType.DMA
    vmem = pltpu.VMEM
    band = (STEPS, LEV, WIN_LAT, COLS, D)
    folded = (STEPS, COUNT, D // 2)
    return pl.pallas_call(
        kernel,
        out_shape=jax.ShapeDtypeStruct(tokens.shape, BF16),
        in_specs=[anywhere] * 8,
        out_specs=anywhere,
        scratch_shapes=[
            vmem(band, BF16),
            vmem(land_sea.shape, jnp.int32),
            vmem(w_qkv.shape, BF16),
            vmem(w_out.shape, BF16),
            vmem((1, D), F32),
            vmem(column.shape, BF16),
            vmem(lane.shape, jnp.int32),
            vmem(lower.shape, F32),
            vmem(folded, BF16),
            vmem(folded, BF16),
            vmem(folded, BF16),
            vmem(folded, BF16),
            vmem((32, 128), BF16),
            vmem((32, 128), BF16),
            vmem((3, COUNT, 128), F32),
            vmem((STEPS, COUNT, D), BF16),
            vmem(band, BF16),
            dma((STEPS,)),
            dma,
            dma((7,)),
            dma((2,)),
            dma((2,)),
            dma((STEPS,)),
            dma((STEPS,)),
            dma((STEPS,)),
            dma((STEPS,)),
            dma((STEPS,)),
            dma((2,)),
        ],
        compiler_params=pltpu.CompilerParams(
            collective_id=0, has_side_effects=True, vmem_limit_bytes=48 * 1024 * 1024
        ),
    )(*[pltpu.with_memory_space_constraint(x, pltpu.HBM) for x in operands])


def solution(mesh):
    in_specs = (P(None, "lat", "lon", None), P(None, "lat", "lon"), P(), P(), P())
    out_specs = P(None, "lat", "lon", None)
    return jax.shard_map(body, mesh=mesh, in_specs=in_specs, out_specs=out_specs, check_vma=False)
```

```python
import functools

import jax
import jax.numpy as jnp
import numpy as np
from jax import lax
from jax.experimental import pallas as pl
from jax.experimental.pallas import tpu as pltpu
from jax.sharding import PartitionSpec as P

HEADS = 8
HEAD = 64
WIN_LAT = 6
WIN_LON = 12
HALF_LAT = 3
HALF_LON = 6
LEV = 2
COLS = 24
D = 512
STEPS = 10
COMBOS = LEV * WIN_LAT
COUNT = COMBOS * WIN_LON
EDGE = COMBOS * HALF_LON
START = 0
AHEAD = 2
RATE = 3
BIG = 1e30
MESH = pl.DeviceIdType.MESH
F32 = jnp.float32
BF16 = jnp.bfloat16


def centre_tokens():
    found = [(n, 8 + s) for n in range(COMBOS) for s in range(8)]
    for m in range(COMBOS // 2):
        found += [(2 * m, 16), (2 * m, 17), (2 * m + 1, 16), (2 * m + 1, 17)]
        found += [(2 * m + 1, 6), (2 * m + 1, 7), (2 * m, 6), (2 * m, 7)]
    return found


def left_tokens():
    found = []
    for n in range(9):
        k = n % 3
        found += [(n, s) for s in range(6)] + [(9 + n // 3, 2 * k), (9 + n // 3, 2 * k + 1)]
    return found


def right_tokens():
    found = []
    for n in range(9):
        k = n % 3
        found += [(9 + n // 3, 18 + 2 * k), (9 + n // 3, 19 + 2 * k)] + [(n, 16 + s) for s in range(2, 8)]
    return found


def tables():
    split = [(n, c - HALF_LON) for n, c in right_tokens()] + [(n, c + 18) for n, c in left_tokens()]
    both = [(n, c - HALF_LON) for n, c in centre_tokens()] + split
    column = np.zeros((2 * COUNT, 32), np.float32)
    lane = np.zeros((2 * COUNT, 128), np.int32)
    lower = np.zeros((2 * COUNT, 128), np.float32)
    for t, (n, c) in enumerate(both):
        level, row = divmod(n, WIN_LAT)
        column[t, c] = 1.0
        lane[t] = np.arange(128) - (64 * level + row)
        lower[t] = 3.0 if row >= HALF_LAT else 0.0
    return column.astype(jnp.bfloat16), lane, lower


def dot(a, b):
    return lax.dot_general(a, b, (((1,), (0,)), ((), ())), preferred_element_type=F32)


def dot_t(a, b):
    return lax.dot_general(a, b, (((1,), (1,)), ((), ())), preferred_element_type=F32)


def rows_of(shape):
    return lax.broadcasted_iota(jnp.int32, shape, 0)


def lanes_of(shape):
    return lax.broadcasted_iota(jnp.int32, shape, 1)


def roll(x, by):
    return pltpu.roll(x, by, 0)


def attend(q, hot, k, far, v):
    n = q.shape[0]
    first = lanes_of((n, 128)) < HEAD
    keep0 = jnp.where(lanes_of((1, 128)) < HEAD, 1.0 / HEAD**0.5, 0.0)
    keep1 = jnp.where(lanes_of((1, 128)) < HEAD, 0.0, 1.0 / HEAD**0.5)
    hot2 = jnp.concatenate([hot, hot], axis=0).astype(BF16)
    ones = jnp.ones((COUNT, 128), BF16)
    found = []
    for pair in range(HEADS // 2):
        cut = slice(128 * pair, 128 * pair + 128)
        part = q[:, cut]
        q2 = jnp.concatenate([part * keep0, part * keep1], axis=0).astype(BF16)
        scores = dot_t(jnp.concatenate([q2, hot2], axis=1), jnp.concatenate([k[:, cut], far], axis=1))
        top = jnp.max(scores, axis=1, keepdims=True)
        expo = jnp.exp(scores - top).astype(BF16)
        summed = dot(expo, jnp.concatenate([v[:, cut], ones], axis=1))
        top_part = jnp.where(first, summed[:n, :128], summed[n:, :128])
        found.append(top_part / jnp.where(first, summed[:n, 128:], summed[n:, 128:]))
    return jnp.concatenate(found, axis=1)


def finish(x, att, w_out, gain):
    proj = dot(att.astype(BF16), w_out)
    centre = proj - jnp.mean(proj, axis=1, keepdims=True)
    spread = jnp.mean(centre * centre, axis=1, keepdims=True)
    return x + gain * (centre * lax.rsqrt(spread + 1e-05))


def features(spread, lane, lower, step, edge):
    surface = jnp.sum(jnp.where(lane == WIN_LAT * step, spread, 0.0), axis=1, keepdims=True)
    same = surface + lower * edge == lanes_of((COUNT, 128)).astype(F32)
    return jnp.where(same, 1.0, 0.0), jnp.where(same, 0.0, -BIG).astype(BF16)


def fold(x):
    return jnp.concatenate([x[:, : D // 2], x[:, D // 2 :]], axis=0).astype(BF16)


def unfold(x):
    x = x.astype(F32)
    return jnp.concatenate([x[:EDGE], x[EDGE:]], axis=1)


def kernel(
    tokens, land, w_qkv, w_out, gain, column, lane, lower, out,
    xs, land_v, wq_v, wo_v, gain_v, column_v, lane_v, lower_v,
    to_west, to_east, from_west, from_east, mine, theirs, spread, centre, res,
    x_sem, x9_sem, in_sem, lat_sem, land_sem, west_send, west_recv, east_send, east_recv, out_sem, back_sem,
):
    lon, lat = lax.axis_index("lon"), lax.axis_index("lat")
    nlon, nlat = lax.axis_size("lon"), lax.axis_size("lat")
    west = (lax.rem(lon + nlon - 1, nlon), lat)
    east = (lax.rem(lon + 1, nlon), lat)
    north = (lon, lax.rem(lat + nlat - 1, nlat))
    south = (lon, lax.rem(lat + 1, nlat))
    last = jnp.where(lat == nlat - 1, 1.0, 0.0)

    barrier = pltpu.get_barrier_semaphore()
    for near in (west, east, north, south):
        pl.semaphore_signal(barrier, inc=1, device_id=near, device_id_type=MESH)

    def x_copy(a):
        return pltpu.make_async_copy(tokens.at[:, pl.ds(WIN_LAT * a + HALF_LAT, WIN_LAT)], xs.at[a], x_sem.at[a])

    x9_copy = pltpu.make_async_copy(
        tokens.at[:, WIN_LAT * STEPS - HALF_LAT : WIN_LAT * STEPS], xs.at[STEPS - 1, :, 0:HALF_LAT], x9_sem
    )
    ins = [
        pltpu.make_async_copy(src, dst, in_sem.at[i])
        for i, (src, dst) in enumerate(
            [(land, land_v), (column, column_v), (lane, lane_v), (lower, lower_v), (gain, gain_v), (w_qkv, wq_v), (w_out, wo_v)]
        )
    ]

    def remote(src, dst, send, recv, device):
        return pltpu.make_async_remote_copy(
            src_ref=src, dst_ref=dst, send_sem=send, recv_sem=recv, device_id=device, device_id_type=MESH
        )

    lat_copy = remote(tokens.at[:, 0:HALF_LAT], xs.at[STEPS - 1, :, HALF_LAT:WIN_LAT], lat_sem.at[0], lat_sem.at[1], north)
    land_copy = remote(mine, theirs, land_sem.at[0], land_sem.at[1], east)
    back_copy = remote(res.at[STEPS - 1, :, HALF_LAT:WIN_LAT], out.at[:, 0:HALF_LAT], back_sem.at[0], back_sem.at[1], south)

    def west_copy(a):
        return remote(to_west.at[a], from_east.at[a], west_send.at[a], west_recv.at[a], west)

    def east_copy(a):
        return remote(to_east.at[a], from_west.at[a], east_send.at[a], east_recv.at[a], east)

    def out_copy(a):
        return pltpu.make_async_copy(res.at[a], out.at[:, pl.ds(WIN_LAT * a + HALF_LAT, WIN_LAT)], out_sem.at[a])

    out9_copy = pltpu.make_async_copy(
        res.at[STEPS - 1, :, 0:HALF_LAT], out.at[:, WIN_LAT * STEPS - HALF_LAT : WIN_LAT * STEPS], out_sem.at[STEPS - 1]
    )

    for i in range(STEPS):
        a = (i + START) % STEPS
        if a == STEPS - 1:
            x9_copy.start()
        else:
            x_copy(a).start()
        if i == 0:
            for copy in ins:
                copy.start()
    pl.semaphore_wait(barrier, 4)
    lat_copy.start()

    row8 = rows_of((8, D))

    def tile(a, n, c):
        return xs[a, n // WIN_LAT, n % WIN_LAT, 8 * c : 8 * c + 8, :].astype(F32)

    def send(a):
        t0 = [tile(a, n, 0) for n in range(COMBOS)]
        t2 = [tile(a, n, 2) for n in range(COMBOS)]
        left = [jnp.where(row8 < 6, t0[n], roll(t0[9 + n // 3], 6 - 2 * (n % 3))) for n in range(9)]
        right = [jnp.where(row8 >= 2, t2[n], roll(t2[9 + n // 3], 6 - 2 * (n % 3))) for n in range(9)]
        to_west[a] = fold(jnp.concatenate(left, axis=0))
        to_east[a] = fold(jnp.concatenate(right, axis=0))
        west_copy(a).start()
        east_copy(a).start()

    def centre_x(a):
        t0 = [tile(a, n, 0) for n in range(COMBOS)]
        t2 = [tile(a, n, 2) for n in range(COMBOS)]
        parts = [tile(a, n, 1) for n in range(COMBOS)]
        for m in range(COMBOS // 2):
            low = jnp.where(row8 < 2, t2[2 * m], roll(t2[2 * m + 1], 2))
            high = jnp.where(row8 < 6, roll(t0[2 * m + 1], 6), t0[2 * m])
            parts.append(jnp.where(row8 < 4, low, high))
        return jnp.concatenate(parts, axis=0)

    def whole(*bands):
        x = jnp.concatenate([centre_x(a) for a in bands], axis=0)
        qkv = dot(x.astype(BF16), wq_v[...])
        att = []
        for d, a in enumerate(bands):
            part = qkv[COUNT * d : COUNT * d + COUNT]
            edge = last * jnp.where(a == STEPS - 1, 1.0, 0.0)
            hot, far = features(spread[0], lane_v[:COUNT], lower_v[:COUNT], a, edge)
            att.append(attend(part[:, :D], hot, part[:, D : 2 * D].astype(BF16), far, part[:, 2 * D :].astype(BF16)))
        y = finish(x, jnp.concatenate(att, axis=0), wo_v[...], gain_v[...]).astype(BF16)
        for d, a in enumerate(bands):
            centre[a] = y[COUNT * d : COUNT * d + COUNT]

    def split(*bands):
        own, keys = [], []
        for a in bands:
            left, right = unfold(to_west[a]), unfold(to_east[a])
            keys.append(jnp.concatenate([unfold(from_west[a]), left], axis=0).astype(BF16))
            keys.append(jnp.concatenate([right, unfold(from_east[a])], axis=0).astype(BF16))
            own += [left, right]
        x = jnp.concatenate(own, axis=0)
        q = dot(x.astype(BF16), wq_v[:, :D])
        kv = dot(jnp.concatenate(keys, axis=0), wq_v[:, D:]).astype(BF16)
        lanes, lowers = lane_v[COUNT:], lower_v[COUNT:]
        att = []
        for d, a in enumerate(bands):
            edge = last * jnp.where(a == STEPS - 1, 1.0, 0.0)
            for w in range(2):
                hot, far = features(spread[1 + w], lanes, lowers, a, edge)
                hot = hot[EDGE:] if w == 0 else hot[:EDGE]
                part = kv[COUNT * (2 * d + w) : COUNT * (2 * d + w + 1)]
                att.append(attend(q[EDGE * (2 * d + w) : EDGE * (2 * d + w + 1)], hot, part[:, :D], far, part[:, D:]))
        y = finish(x, jnp.concatenate(att, axis=0), wo_v[...], gain_v[...])
        for d, a in enumerate(bands):
            assemble(a, y[COUNT * d : COUNT * d + COUNT])

    def assemble(a, y):
        lefts = [y[8 * n : 8 * n + 8] for n in range(9)]
        rights = [y[EDGE + 8 * n : EDGE + 8 * n + 8] for n in range(9)]
        mid = centre[a].astype(F32)
        for n in range(COMBOS):
            rest = mid[96 + 8 * (n // 2) : 104 + 8 * (n // 2)]
            rest0, rest2 = (rest, rest) if n % 2 == 0 else (roll(rest, 2), roll(rest, 6))
            if n < 9:
                tile0 = jnp.where(row8 < 6, lefts[n], rest0)
                tile2 = jnp.where(row8 >= 2, rights[n], rest2)
            else:
                b = 3 * (n - 9)
                low = jnp.where(row8 < 2, roll(lefts[b], 2), roll(lefts[b + 1], 4))
                tile0 = jnp.where(row8 < 4, low, jnp.where(row8 < 6, roll(lefts[b + 2], 6), rest0))
                low = jnp.where(row8 < 2, rest2, roll(rights[b], 2))
                tile2 = jnp.where(row8 < 4, low, jnp.where(row8 < 6, roll(rights[b + 1], 4), roll(rights[b + 2], 6)))
            whole_row = jnp.concatenate([tile0, mid[8 * n : 8 * n + 8], tile2], axis=0)
            res[a, n // WIN_LAT, n % WIN_LAT] = whole_row.astype(BF16)

    nine = (STEPS - 1 - START) // 2

    def early(i):
        send(lax.rem(i + START, STEPS - 1))

    for d in range(2):
        x_copy(d + START).wait()
        early(d)

    def loaded(i, carry):
        x_copy(lax.rem(i + START, STEPS - 1)).wait()
        return carry

    lax.fori_loop(2, STEPS - 1, loaded, 0)

    for copy in ins[:4]:
        copy.wait()
    across = jnp.zeros((COLS, 128), F32)
    rows = land_v.shape[2]
    for level in range(LEV):
        place = rows_of((rows, 128)) + 64 * level == lanes_of((rows, 128))
        across += dot(land_v[level].astype(F32).astype(BF16), jnp.where(place, 1.0, 0.0).astype(BF16))
    mine[...] = jnp.concatenate([across, jnp.zeros((32 - COLS, 128), F32)], axis=0).astype(BF16)
    land_copy.start()
    spread[0] = dot(column_v[:COUNT], mine[...])
    spread[2] = dot(column_v[COUNT:], mine[...])
    for copy in ins[4:]:
        copy.wait()

    def pair(i):
        return [lax.rem(2 * i + d + START, STEPS) for d in range(2)]

    def more_sends(slot):
        for d in range(RATE):

            @pl.when(2 + RATE * slot + d < STEPS - 1)
            def _():
                early(2 + RATE * slot + d)

    def ahead(i, carry):
        whole(*pair(i))

        @pl.when(i < AHEAD - 1)
        def _():
            more_sends(i)

        return carry

    lax.fori_loop(0, AHEAD, ahead, 0)
    land_copy.wait()
    spread[1] = dot(column_v[COUNT:], theirs[...])

    def step(i, carry, merged):
        more_sends(i + AHEAD - 1)
        if merged == 1:

            @pl.when(i == nine - 1)
            def _():
                x9_copy.wait()
                lat_copy.wait()
                send(STEPS - 1)

        bands = pair(i)
        for a in bands:
            west_copy(a).wait()
            east_copy(a).wait()
        split(*bands)
        if merged:
            whole(*pair(i + merged))
        for a in bands:

            @pl.when(a == STEPS - 1)
            def _():
                back_copy.start()
                out9_copy.start()

            @pl.when(a != STEPS - 1)
            def _():
                out_copy(a).start()

        return carry

    lax.fori_loop(0, nine - AHEAD, functools.partial(step, merged=AHEAD), 0)
    lax.fori_loop(nine - AHEAD, nine - 1, functools.partial(step, merged=0), 0)
    lax.fori_loop(nine - 1, nine, functools.partial(step, merged=1), 0)
    lax.fori_loop(nine, STEPS // 2, functools.partial(step, merged=0), 0)

    def drain(a, carry):
        out_copy(a).wait()
        return carry

    lax.fori_loop(0, STEPS - 1, drain, 0)
    out9_copy.wait()
    back_copy.wait()


def body(tokens, land_sea, w_qkv, w_out, norm_gain):
    column, lane, lower = tables()
    land_sea = jnp.transpose(land_sea, (0, 2, 1))
    anywhere = pl.BlockSpec(memory_space=pl.ANY)
    operands = (tokens, land_sea, w_qkv, w_out, norm_gain.reshape(1, D), column, lane, lower)
    dma = pltpu.SemaphoreType.DMA
    vmem = pltpu.VMEM
    band = (STEPS, LEV, WIN_LAT, COLS, D)
    folded = (STEPS, COUNT, D // 2)
    return pl.pallas_call(
        kernel,
        out_shape=jax.ShapeDtypeStruct(tokens.shape, BF16),
        in_specs=[anywhere] * 8,
        out_specs=anywhere,
        scratch_shapes=[
            vmem(band, BF16),
            vmem(land_sea.shape, jnp.int32),
            vmem(w_qkv.shape, BF16),
            vmem(w_out.shape, BF16),
            vmem((1, D), F32),
            vmem(column.shape, BF16),
            vmem(lane.shape, jnp.int32),
            vmem(lower.shape, F32),
            vmem(folded, BF16),
            vmem(folded, BF16),
            vmem(folded, BF16),
            vmem(folded, BF16),
            vmem((32, 128), BF16),
            vmem((32, 128), BF16),
            vmem((3, COUNT, 128), F32),
            vmem((STEPS, COUNT, D), BF16),
            vmem(band, BF16),
            dma((STEPS,)),
            dma,
            dma((7,)),
            dma((2,)),
            dma((2,)),
            dma((STEPS,)),
            dma((STEPS,)),
            dma((STEPS,)),
            dma((STEPS,)),
            dma((STEPS,)),
            dma((2,)),
        ],
        compiler_params=pltpu.CompilerParams(
            collective_id=0, has_side_effects=True, vmem_limit_bytes=48 * 1024 * 1024
        ),
    )(*[pltpu.with_memory_space_constraint(x, pltpu.HBM) for x in operands])


def solution(mesh):
    in_specs = (P(None, "lat", "lon", None), P(None, "lat", "lon"), P(), P(), P())
    out_specs = P(None, "lat", "lon", None)
    return jax.shard_map(body, mesh=mesh, in_specs=in_specs, out_specs=out_specs, check_vma=False)
```

```python
import functools

import jax
import jax.numpy as jnp
import numpy as np
from jax import lax
from jax.experimental import pallas as pl
from jax.experimental.pallas import tpu as pltpu
from jax.sharding import PartitionSpec as P

HEADS = 8
HEAD = 64
WIN_LAT = 6
WIN_LON = 12
HALF_LAT = 3
HALF_LON = 6
LEV = 2
COLS = 24
D = 512
STEPS = 10
COMBOS = LEV * WIN_LAT
COUNT = COMBOS * WIN_LON
EDGE = COMBOS * HALF_LON
START = 0
AHEAD = 2
RATE = 3
RING = 4
HOLD = 1
BIG = 1e30
MESH = pl.DeviceIdType.MESH
F32 = jnp.float32
BF16 = jnp.bfloat16


def centre_tokens():
    found = [(n, 8 + s) for n in range(COMBOS) for s in range(8)]
    for m in range(COMBOS // 2):
        found += [(2 * m, 16), (2 * m, 17), (2 * m + 1, 16), (2 * m + 1, 17)]
        found += [(2 * m + 1, 6), (2 * m + 1, 7), (2 * m, 6), (2 * m, 7)]
    return found


def left_tokens():
    found = []
    for n in range(9):
        k = n % 3
        found += [(n, s) for s in range(6)] + [(9 + n // 3, 2 * k), (9 + n // 3, 2 * k + 1)]
    return found


def right_tokens():
    found = []
    for n in range(9):
        k = n % 3
        found += [(9 + n // 3, 18 + 2 * k), (9 + n // 3, 19 + 2 * k)] + [(n, 16 + s) for s in range(2, 8)]
    return found


def tables():
    split = [(n, c - HALF_LON) for n, c in right_tokens()] + [(n, c + 18) for n, c in left_tokens()]
    both = [(n, c - HALF_LON) for n, c in centre_tokens()] + split
    column = np.zeros((2 * COUNT, 32), np.float32)
    lane = np.zeros((2 * COUNT, 128), np.int32)
    lower = np.zeros((2 * COUNT, 128), np.float32)
    for t, (n, c) in enumerate(both):
        level, row = divmod(n, WIN_LAT)
        column[t, c] = 1.0
        lane[t] = np.arange(128) - (64 * level + row)
        lower[t] = 3.0 if row >= HALF_LAT else 0.0
    return column.astype(jnp.bfloat16), lane, lower


def dot(a, b):
    return lax.dot_general(a, b, (((1,), (0,)), ((), ())), preferred_element_type=F32)


def dot_t(a, b):
    return lax.dot_general(a, b, (((1,), (1,)), ((), ())), preferred_element_type=F32)


def rows_of(shape):
    return lax.broadcasted_iota(jnp.int32, shape, 0)


def lanes_of(shape):
    return lax.broadcasted_iota(jnp.int32, shape, 1)


def roll(x, by):
    return pltpu.roll(x, by, 0)


def attend(q, hot, k, far, v):
    n = q.shape[0]
    first = lanes_of((n, 128)) < HEAD
    keep0 = jnp.where(lanes_of((1, 128)) < HEAD, 1.0 / HEAD**0.5, 0.0)
    keep1 = jnp.where(lanes_of((1, 128)) < HEAD, 0.0, 1.0 / HEAD**0.5)
    hot2 = jnp.concatenate([hot, hot], axis=0).astype(BF16)
    ones = jnp.ones((COUNT, 128), BF16)
    found = []
    for pair in range(HEADS // 2):
        cut = slice(128 * pair, 128 * pair + 128)
        part = q[:, cut]
        q2 = jnp.concatenate([part * keep0, part * keep1], axis=0).astype(BF16)
        scores = dot_t(jnp.concatenate([q2, hot2], axis=1), jnp.concatenate([k[:, cut], far], axis=1))
        top = jnp.max(scores, axis=1, keepdims=True)
        expo = jnp.exp(scores - top).astype(BF16)
        summed = dot(expo, jnp.concatenate([v[:, cut], ones], axis=1))
        top_part = jnp.where(first, summed[:n, :128], summed[n:, :128])
        found.append(top_part / jnp.where(first, summed[:n, 128:], summed[n:, 128:]))
    return jnp.concatenate(found, axis=1)


def finish(x, att, w_out, gain):
    proj = dot(att.astype(BF16), w_out)
    centre = proj - jnp.mean(proj, axis=1, keepdims=True)
    spread = jnp.mean(centre * centre, axis=1, keepdims=True)
    return x + gain * (centre * lax.rsqrt(spread + 1e-05))


def features(spread, lane, lower, step, edge):
    surface = jnp.sum(jnp.where(lane == WIN_LAT * step, spread, 0.0), axis=1, keepdims=True)
    same = surface + lower * edge == lanes_of((COUNT, 128)).astype(F32)
    return jnp.where(same, 1.0, 0.0), jnp.where(same, 0.0, -BIG).astype(BF16)


def fold(x):
    return jnp.concatenate([x[:, : D // 2], x[:, D // 2 :]], axis=0).astype(BF16)


def unfold(x):
    x = x.astype(F32)
    return jnp.concatenate([x[:EDGE], x[EDGE:]], axis=1)


def kernel(
    tokens, land, w_qkv, w_out, gain, column, lane, lower, out,
    xs, land_v, wq_v, wo_v, gain_v, column_v, lane_v, lower_v,
    to_west, to_east, from_west, from_east, mine, theirs, spread, centre, res,
    x_sem, x9_sem, in_sem, lat_sem, land_sem, west_send, west_recv, east_send, east_recv, out_sem, back_sem,
):
    lon, lat = lax.axis_index("lon"), lax.axis_index("lat")
    nlon, nlat = lax.axis_size("lon"), lax.axis_size("lat")
    west = (lax.rem(lon + nlon - 1, nlon), lat)
    east = (lax.rem(lon + 1, nlon), lat)
    north = (lon, lax.rem(lat + nlat - 1, nlat))
    south = (lon, lax.rem(lat + 1, nlat))
    last = jnp.where(lat == nlat - 1, 1.0, 0.0)

    barrier = pltpu.get_barrier_semaphore()
    for near in (west, east, north, south):
        pl.semaphore_signal(barrier, inc=1, device_id=near, device_id_type=MESH)

    def x_copy(a):
        return pltpu.make_async_copy(tokens.at[:, pl.ds(WIN_LAT * a + HALF_LAT, WIN_LAT)], xs.at[a], x_sem.at[a])

    x9_copy = pltpu.make_async_copy(
        tokens.at[:, WIN_LAT * STEPS - HALF_LAT : WIN_LAT * STEPS], xs.at[STEPS - 1, :, 0:HALF_LAT], x9_sem
    )
    ins = [
        pltpu.make_async_copy(src, dst, in_sem.at[i])
        for i, (src, dst) in enumerate(
            [(land, land_v), (column, column_v), (lane, lane_v), (lower, lower_v), (gain, gain_v), (w_qkv, wq_v), (w_out, wo_v)]
        )
    ]

    def remote(src, dst, send, recv, device):
        return pltpu.make_async_remote_copy(
            src_ref=src, dst_ref=dst, send_sem=send, recv_sem=recv, device_id=device, device_id_type=MESH
        )

    lat_copy = remote(tokens.at[:, 0:HALF_LAT], xs.at[STEPS - 1, :, HALF_LAT:WIN_LAT], lat_sem.at[0], lat_sem.at[1], north)
    land_copy = remote(mine, theirs, land_sem.at[0], land_sem.at[1], east)
    back_copy = remote(res.at[STEPS - 1, :, HALF_LAT:WIN_LAT], out.at[:, 0:HALF_LAT], back_sem.at[0], back_sem.at[1], south)

    def west_copy(a):
        return remote(to_west.at[a], from_east.at[a], west_send.at[a], west_recv.at[a], west)

    def east_copy(a):
        return remote(to_east.at[a], from_west.at[a], east_send.at[a], east_recv.at[a], east)

    def out_copy(a):
        return pltpu.make_async_copy(res.at[a], out.at[:, pl.ds(WIN_LAT * a + HALF_LAT, WIN_LAT)], out_sem.at[a])

    out9_copy = pltpu.make_async_copy(
        res.at[STEPS - 1, :, 0:HALF_LAT], out.at[:, WIN_LAT * STEPS - HALF_LAT : WIN_LAT * STEPS], out_sem.at[STEPS - 1]
    )

    for i in range(STEPS):
        a = (i + START) % STEPS
        if a == STEPS - 1:
            x9_copy.start()
        else:
            x_copy(a).start()
        if i == 0:
            for copy in ins:
                copy.start()
    pl.semaphore_wait(barrier, 4)
    lat_copy.start()

    row8 = rows_of((8, D))
    hold_east = lax.rem(lon, 2 * RING) == RING - 1
    hold_west = lax.rem(lon, 2 * RING) == RING

    def tile(a, n, c):
        return xs[a, n // WIN_LAT, n % WIN_LAT, 8 * c : 8 * c + 8, :].astype(F32)

    def send(a):
        t0 = [tile(a, n, 0) for n in range(COMBOS)]
        t2 = [tile(a, n, 2) for n in range(COMBOS)]
        left = [jnp.where(row8 < 6, t0[n], roll(t0[9 + n // 3], 6 - 2 * (n % 3))) for n in range(9)]
        right = [jnp.where(row8 >= 2, t2[n], roll(t2[9 + n // 3], 6 - 2 * (n % 3))) for n in range(9)]
        to_west[a] = fold(jnp.concatenate(left, axis=0))
        to_east[a] = fold(jnp.concatenate(right, axis=0))
        at_once = a == STEPS - 1

        @pl.when(at_once | ~hold_west)
        def _():
            west_copy(a).start()

        @pl.when(at_once | ~hold_east)
        def _():
            east_copy(a).start()

    def centre_x(a):
        t0 = [tile(a, n, 0) for n in range(COMBOS)]
        t2 = [tile(a, n, 2) for n in range(COMBOS)]
        parts = [tile(a, n, 1) for n in range(COMBOS)]
        for m in range(COMBOS // 2):
            low = jnp.where(row8 < 2, t2[2 * m], roll(t2[2 * m + 1], 2))
            high = jnp.where(row8 < 6, roll(t0[2 * m + 1], 6), t0[2 * m])
            parts.append(jnp.where(row8 < 4, low, high))
        return jnp.concatenate(parts, axis=0)

    def whole(*bands):
        x = jnp.concatenate([centre_x(a) for a in bands], axis=0)
        qkv = dot(x.astype(BF16), wq_v[...])
        att = []
        for d, a in enumerate(bands):
            part = qkv[COUNT * d : COUNT * d + COUNT]
            edge = last * jnp.where(a == STEPS - 1, 1.0, 0.0)
            hot, far = features(spread[0], lane_v[:COUNT], lower_v[:COUNT], a, edge)
            att.append(attend(part[:, :D], hot, part[:, D : 2 * D].astype(BF16), far, part[:, 2 * D :].astype(BF16)))
        y = finish(x, jnp.concatenate(att, axis=0), wo_v[...], gain_v[...]).astype(BF16)
        for d, a in enumerate(bands):
            centre[a] = y[COUNT * d : COUNT * d + COUNT]

    def split(*bands):
        own, keys = [], []
        for a in bands:
            left, right = unfold(to_west[a]), unfold(to_east[a])
            keys.append(jnp.concatenate([unfold(from_west[a]), left], axis=0).astype(BF16))
            keys.append(jnp.concatenate([right, unfold(from_east[a])], axis=0).astype(BF16))
            own += [left, right]
        x = jnp.concatenate(own, axis=0)
        q = dot(x.astype(BF16), wq_v[:, :D])
        kv = dot(jnp.concatenate(keys, axis=0), wq_v[:, D:]).astype(BF16)
        lanes, lowers = lane_v[COUNT:], lower_v[COUNT:]
        att = []
        for d, a in enumerate(bands):
            edge = last * jnp.where(a == STEPS - 1, 1.0, 0.0)
            for w in range(2):
                hot, far = features(spread[1 + w], lanes, lowers, a, edge)
                hot = hot[EDGE:] if w == 0 else hot[:EDGE]
                part = kv[COUNT * (2 * d + w) : COUNT * (2 * d + w + 1)]
                att.append(attend(q[EDGE * (2 * d + w) : EDGE * (2 * d + w + 1)], hot, part[:, :D], far, part[:, D:]))
        y = finish(x, jnp.concatenate(att, axis=0), wo_v[...], gain_v[...])
        for d, a in enumerate(bands):
            assemble(a, y[COUNT * d : COUNT * d + COUNT])

    def assemble(a, y):
        lefts = [y[8 * n : 8 * n + 8] for n in range(9)]
        rights = [y[EDGE + 8 * n : EDGE + 8 * n + 8] for n in range(9)]
        mid = centre[a].astype(F32)
        for n in range(COMBOS):
            rest = mid[96 + 8 * (n // 2) : 104 + 8 * (n // 2)]
            rest0, rest2 = (rest, rest) if n % 2 == 0 else (roll(rest, 2), roll(rest, 6))
            if n < 9:
                tile0 = jnp.where(row8 < 6, lefts[n], rest0)
                tile2 = jnp.where(row8 >= 2, rights[n], rest2)
            else:
                b = 3 * (n - 9)
                low = jnp.where(row8 < 2, roll(lefts[b], 2), roll(lefts[b + 1], 4))
                tile0 = jnp.where(row8 < 4, low, jnp.where(row8 < 6, roll(lefts[b + 2], 6), rest0))
                low = jnp.where(row8 < 2, rest2, roll(rights[b], 2))
                tile2 = jnp.where(row8 < 4, low, jnp.where(row8 < 6, roll(rights[b + 1], 4), roll(rights[b + 2], 6)))
            whole_row = jnp.concatenate([tile0, mid[8 * n : 8 * n + 8], tile2], axis=0)
            res[a, n // WIN_LAT, n % WIN_LAT] = whole_row.astype(BF16)

    nine = (STEPS - 1 - START) // 2

    def early(i):
        send(lax.rem(i + START, STEPS - 1))

    for d in range(2):
        x_copy(d + START).wait()
        early(d)

    def loaded(i, carry):
        x_copy(lax.rem(i + START, STEPS - 1)).wait()
        return carry

    lax.fori_loop(2, STEPS - 1, loaded, 0)

    for copy in ins[:4]:
        copy.wait()
    across = jnp.zeros((COLS, 128), F32)
    rows = land_v.shape[2]
    for level in range(LEV):
        place = rows_of((rows, 128)) + 64 * level == lanes_of((rows, 128))
        across += dot(land_v[level].astype(F32).astype(BF16), jnp.where(place, 1.0, 0.0).astype(BF16))
    mine[...] = jnp.concatenate([across, jnp.zeros((32 - COLS, 128), F32)], axis=0).astype(BF16)
    land_copy.start()
    spread[0] = dot(column_v[:COUNT], mine[...])
    spread[2] = dot(column_v[COUNT:], mine[...])
    for copy in ins[4:]:
        copy.wait()

    def pair(i):
        return [lax.rem(2 * i + d + START, STEPS) for d in range(2)]

    def more_sends(slot):
        for d in range(RATE):

            @pl.when(2 + RATE * slot + d < STEPS - 1)
            def _():
                early(2 + RATE * slot + d)

        for d in range(RATE):
            a = 2 + RATE * (slot - HOLD) + d

            @pl.when((a >= 0) & (a < STEPS - 1) & hold_west)
            def _():
                west_copy(a).start()

            @pl.when((a >= 0) & (a < STEPS - 1) & hold_east)
            def _():
                east_copy(a).start()

    def ahead(i, carry):
        whole(*pair(i))

        @pl.when(i < AHEAD - 1)
        def _():
            more_sends(i)

        return carry

    lax.fori_loop(0, AHEAD, ahead, 0)
    land_copy.wait()
    spread[1] = dot(column_v[COUNT:], theirs[...])

    def step(i, carry, merged):
        more_sends(i + AHEAD - 1)
        if merged == 0:

            @pl.when(i == nine - 2)
            def _():
                x9_copy.wait()
                lat_copy.wait()
                send(STEPS - 1)

        bands = pair(i)
        for a in bands:
            west_copy(a).wait_recv()
            east_copy(a).wait_recv()
        split(*bands)
        if merged:
            whole(*pair(i + merged))
        for a in bands:

            @pl.when(a == STEPS - 1)
            def _():
                back_copy.start()
                out9_copy.start()

            @pl.when(a != STEPS - 1)
            def _():
                out_copy(a).start()

        return carry

    lax.fori_loop(0, nine - AHEAD, functools.partial(step, merged=AHEAD), 0)
    lax.fori_loop(nine - AHEAD, nine - 1, functools.partial(step, merged=0), 0)
    lax.fori_loop(nine - 1, nine, functools.partial(step, merged=1), 0)
    lax.fori_loop(nine, STEPS // 2, functools.partial(step, merged=0), 0)

    def sent(a, carry):
        west_copy(a).wait_send()
        east_copy(a).wait_send()
        return carry

    lax.fori_loop(0, STEPS, sent, 0)

    def drain(a, carry):
        out_copy(a).wait()
        return carry

    lax.fori_loop(0, STEPS - 1, drain, 0)
    out9_copy.wait()
    back_copy.wait()


def body(tokens, land_sea, w_qkv, w_out, norm_gain):
    column, lane, lower = tables()
    land_sea = jnp.transpose(land_sea, (0, 2, 1))
    anywhere = pl.BlockSpec(memory_space=pl.ANY)
    operands = (tokens, land_sea, w_qkv, w_out, norm_gain.reshape(1, D), column, lane, lower)
    dma = pltpu.SemaphoreType.DMA
    vmem = pltpu.VMEM
    band = (STEPS, LEV, WIN_LAT, COLS, D)
    folded = (STEPS, COUNT, D // 2)
    return pl.pallas_call(
        kernel,
        out_shape=jax.ShapeDtypeStruct(tokens.shape, BF16),
        in_specs=[anywhere] * 8,
        out_specs=anywhere,
        scratch_shapes=[
            vmem(band, BF16),
            vmem(land_sea.shape, jnp.int32),
            vmem(w_qkv.shape, BF16),
            vmem(w_out.shape, BF16),
            vmem((1, D), F32),
            vmem(column.shape, BF16),
            vmem(lane.shape, jnp.int32),
            vmem(lower.shape, F32),
            vmem(folded, BF16),
            vmem(folded, BF16),
            vmem(folded, BF16),
            vmem(folded, BF16),
            vmem((32, 128), BF16),
            vmem((32, 128), BF16),
            vmem((3, COUNT, 128), F32),
            vmem((STEPS, COUNT, D), BF16),
            vmem(band, BF16),
            dma((STEPS,)),
            dma,
            dma((7,)),
            dma((2,)),
            dma((2,)),
            dma((STEPS,)),
            dma((STEPS,)),
            dma((STEPS,)),
            dma((STEPS,)),
            dma((STEPS,)),
            dma((2,)),
        ],
        compiler_params=pltpu.CompilerParams(
            collective_id=0, has_side_effects=True, vmem_limit_bytes=48 * 1024 * 1024
        ),
    )(*[pltpu.with_memory_space_constraint(x, pltpu.HBM) for x in operands])


def solution(mesh):
    in_specs = (P(None, "lat", "lon", None), P(None, "lat", "lon"), P(), P(), P())
    out_specs = P(None, "lat", "lon", None)
    return jax.shard_map(body, mesh=mesh, in_specs=in_specs, out_specs=out_specs, check_vma=False)
```
